32 devices in a mesh: groups: 2 (over y), replica: 4 (over x, core), tensor: 4 (over z).
Axes of the slice: x: 2, y: 2, z: 4, core: 2. Of those that a mesh axis runs over, the one named last changes fastest.
Arguments:
- tokens: bfloat16 [4096, 8192], P(('groups', 'replica'), 'tensor'), parts along dimension 0, may hold values from -6 to 6
- query_weight: bfloat16 [8192, 4096], P(None, 'tensor'), may hold values from -0.0625 to 0.0625
- adapter_down: bfloat16 [64, 8192, 64], P('replica', 'tensor'), may hold values from -0.0625 to 0.0625
- adapter_up: bfloat16 [64, 64, 4096], P('replica', None, 'tensor'), may hold values from -0.75 to 0.75
- send_table: int32 [8, 4, 2], P('groups'), parts along dimension 0, may hold values from 0 to 15, as said below
- block_slot: int32 [128], P(('groups', 'replica')), parts along dimension 0, may hold values from 0 to 7, as said below
- live_block_rows: int32 [128], P(('groups', 'replica')), parts along dimension 0, may hold values from 1 to 32, as said below
Outputs:
- queries: bfloat16 [4096, 4096], P(('groups', 'replica'), 'tensor'), parts along dimension 0
The draws below stay inside these ranges and needn't reach their ends.
There are 2 independent parts, one for each index of `groups`. The reference program is written for one: setup_inputs(seed, part) draws one part's arguments, and reference() takes and returns one part's arrays. A program takes and returns all parts, laid end to end along the dimension named above; an argument that names none is the same for every part. Nothing has to cross between parts.
Inputs may be any that keep to these rules, and one draw needn't show every extreme that they name: send_table[o, r, c] names adapter o * 16 + value. `block_slot`: block k uses the piece that owner replica value // 2 sends to replica k // 16 in slot value % 2. `live_block_rows`: rows past this count in a block are padding.
All inputs are finite; a program needn't handle non-finite values.
Results may differ from the reference program's by a relative error of at most 0.0034.
Values may be sent and summed in bfloat16 or wider, within the bound.
A program may use at most 128 MiB of HBM per device.

```python
import jax
import jax.numpy as jnp

D = 8192
DQ = 4096
RANK = 64
ADP_REP = 16
BLK = 32
CAP = 2
NBLK = 16
ADAPTERS = 64
ROWS = 2048
N_REPLICA = 4


def draw_send_table(key, part):
    key = jax.random.fold_in(key, 11)
    first_key, second_key, third_key, order_key = jax.random.split(key, 4)
    shape = (N_REPLICA, N_REPLICA, CAP)
    first = jax.random.randint(first_key, shape, 0, ADP_REP)
    second = jax.random.randint(second_key, shape, 0, ADP_REP)
    third = jax.random.randint(third_key, shape, 0, ADP_REP)
    picked = jnp.minimum(jnp.minimum(first, second), third)
    order = jax.random.permutation(order_key, ADP_REP)
    table = order[picked]
    flat = jnp.arange(N_REPLICA * N_REPLICA * CAP, dtype=jnp.int32).reshape(shape)
    table = jnp.where(flat == 0, ADP_REP - 1, table)
    return table.astype(jnp.int32)


def draw_block_slot(key, part):
    key = jax.random.fold_in(key, 23)
    count = NBLK * N_REPLICA
    values = jax.random.randint(key, (count,), 0, N_REPLICA * CAP)
    values = jnp.where(jnp.arange(count, dtype=jnp.int32) == 0, N_REPLICA * CAP - 1, values)
    return values.astype(jnp.int32)


def draw_live_block_rows(key, part):
    key = jax.random.fold_in(key, 37)
    count = NBLK * N_REPLICA
    values = jax.random.randint(key, (count,), 1, BLK + 1)
    values = jnp.where(jnp.arange(count, dtype=jnp.int32) % NBLK == 0, BLK, values)
    return values.astype(jnp.int32)


def level_of(rng, dims, pieces, least, largest):
    level, own = 1.0, jax.random.fold_in(rng, 6)
    for axis_at, parts in pieces:
        draws = jnp.exp(jax.random.uniform(jax.random.fold_in(own, axis_at), (parts,), jnp.float32, least / len(pieces), largest / len(pieces)))
        level = level * jnp.repeat(draws, dims[axis_at] // parts).reshape([-1 if axis == axis_at else 1 for axis in range(len(dims))])
    return level


def gaussian(own_key, extent, spread, limit, cuts=(), kind=jnp.bfloat16):
    result = spread * jax.random.normal(own_key, extent, jnp.float32)
    if cuts:
        result = result * level_of(own_key, extent, cuts, -0.22, 0.18)
    return jnp.clip(result, -limit, limit).astype(kind)


def setup_inputs(seed: int = 0, part: int = 0) -> dict:
    keys = jax.random.split(jax.random.key(seed), 8)
    part_keys = jax.random.split(jax.random.fold_in(keys[7], part), 8)
    tokens = gaussian(part_keys[0], (ROWS, D), 1.0, 6.0, ((0, 4), (1, 4)))
    query_weight = gaussian(keys[1], (D, DQ), D ** -0.5, 0.0625, ((1, 4),))
    adapter_down = gaussian(keys[2], (ADAPTERS, D, RANK), D ** -0.5, 0.0625, ((0, 4), (1, 4)))
    adapter_up = gaussian(keys[3], (ADAPTERS, RANK, DQ), RANK ** -0.5, 0.75, ((0, 4), (2, 4)))
    send_table = draw_send_table(jax.random.fold_in(jax.random.fold_in(keys[7], part), 71), part)
    block_slot = draw_block_slot(jax.random.fold_in(jax.random.fold_in(keys[7], part), 71), part)
    live_block_rows = draw_live_block_rows(jax.random.fold_in(jax.random.fold_in(keys[7], part), 71), part)
    return {"tokens": tokens, "query_weight": query_weight, "adapter_down": adapter_down, "adapter_up": adapter_up, "send_table": send_table, "block_slot": block_slot, "live_block_rows": live_block_rows}


def reference(tokens, query_weight, adapter_down, adapter_up, send_table, block_slot, live_block_rows):
    count = block_slot.shape[0]
    serving = jnp.arange(count, dtype=jnp.int32) // NBLK
    owner = block_slot // CAP
    slot = block_slot % CAP
    adapter = (owner * ADP_REP + send_table[owner, serving, slot]).astype(jnp.int32)
    base = jnp.dot(tokens, query_weight, preferred_element_type=jnp.float32)
    block_list = tokens.reshape(count, BLK, D).astype(jnp.float32)
    down_weight_selected = adapter_down[adapter].astype(jnp.float32)
    shrink_rank = jnp.einsum("zlc,zcx->zlx", block_list, down_weight_selected)
    shrink_round = shrink_rank.astype(jnp.bfloat16).astype(jnp.float32)
    up_sel = adapter_up[adapter].astype(jnp.float32)
    delta = jnp.einsum("bkr,brc->bkc", shrink_round, up_sel)
    live = (jnp.arange(BLK, dtype=jnp.int32)[None, :] < live_block_rows[:, None]).astype(jnp.float32)
    delta = delta * live[:, :, None]
    return (base + delta.reshape(count * BLK, DQ)).astype(jnp.bfloat16)
```

```python
import jax
import jax.numpy as jnp
from jax import lax
from jax.sharding import PartitionSpec as P

CHUNKS = 4


def exchange_adapters(adapter_down, adapter_up, send_table):
    me = lax.axis_index("replica")
    count = lax.axis_size("replica")
    downs, ups = [], []
    for k in range(count):
        wanted = send_table[me, me ^ k]
        down = adapter_down[wanted]
        up = adapter_up[wanted]
        if k:
            perm = [(i, i ^ k) for i in range(count)]
            down = lax.ppermute(down, "replica", perm)
            up = lax.ppermute(up, "replica", perm)
        downs.append(down)
        ups.append(up)
    return downs, ups


def adapter_term(tokens, adapter_down, adapter_up, send_table, block_slot, live_block_rows):
    count = live_block_rows.shape[0]
    block_rows = tokens.shape[0] // count
    slots_each = send_table.shape[2]
    rank = adapter_down.shape[2]
    me = lax.axis_index("replica")
    downs, ups = exchange_adapters(adapter_down, adapter_up, send_table)
    place = ((block_slot // slots_each) ^ me) * slots_each + block_slot % slots_each
    row_place = jnp.repeat(place, block_rows)
    partial = jnp.zeros((tokens.shape[0], rank), jnp.float32)
    for k, down in enumerate(downs):
        product = jnp.einsum("rd,cdx->rcx", tokens, down, preferred_element_type=jnp.float32)
        for c in range(slots_each):
            partial = jnp.where((row_place == k * slots_each + c)[:, None], product[:, c], partial)
    shrink_round = lax.psum(partial, "tensor").astype(jnp.bfloat16)
    live = jnp.arange(block_rows, dtype=jnp.int32)[None, :] < live_block_rows[:, None]
    live = live.reshape(-1)
    pieces = len(downs) * slots_each
    spread = jnp.where(
        (live[:, None] & (row_place[:, None] == jnp.arange(pieces, dtype=jnp.int32)[None, :]))[:, :, None],
        shrink_round[:, None, :],
        jnp.bfloat16(0),
    ).reshape(tokens.shape[0], pieces * rank)
    up_all = jnp.concatenate(ups, axis=0).reshape(pieces * rank, -1)
    return jnp.dot(spread, up_all, preferred_element_type=jnp.float32)


def shards_any(tokens, query_weight, adapter_down, adapter_up, send_table, block_slot, live_block_rows):
    delta = adapter_term(tokens, adapter_down, adapter_up, send_table, block_slot, live_block_rows)
    base = jnp.dot(
        lax.all_gather(tokens, "tensor", axis=1, tiled=True),
        query_weight,
        preferred_element_type=jnp.float32,
    )
    return (base + delta).astype(jnp.bfloat16)


def dot(a, b):
    return jnp.dot(a, b, preferred_element_type=jnp.float32)


def shards_line4(tokens, query_weight, adapter_down, adapter_up, send_table, block_slot, live_block_rows):
    t = lax.axis_index("tensor")
    rows, depth = tokens.shape
    step = rows // CHUNKS
    right = [(0, 1), (1, 2), (2, 3)]
    left = [(1, 0), (2, 1), (3, 2)]
    swap = [(1, 2), (2, 1)]

    near_at = jnp.where(t < 2, 2, 1)
    far_at = jnp.where(t < 2, 3, 0)
    peers = lax.axis_size("groups") * lax.axis_size("replica")
    peer = lax.axis_index(("groups", "replica"))
    each = 2 * depth // peers
    half = peers // 2
    start = jnp.where(peer < half, near_at, far_at) * depth + (peer % half) * each
    piece = lax.dynamic_slice_in_dim(query_weight, start, each, 0)
    piece = lax.ppermute(piece, "tensor", [(0, 1), (3, 2)])
    help_weight = lax.all_gather(piece, ("groups", "replica"), axis=0, tiled=True)

    delta = adapter_term(tokens, adapter_down, adapter_up, send_table, block_slot, live_block_rows)

    def weight_rows(i):
        return lax.dynamic_slice_in_dim(query_weight, jnp.clip(i, 0, 3) * depth, depth, 0)

    own_w = weight_rows(t)
    left_w = weight_rows(t - 1)
    right_w = weight_rows(t + 1)
    distant_w = weight_rows(jnp.where(t < 2, t + 2, t - 2))

    outs = []
    for c in range(CHUNKS):
        mine = tokens[c * step : (c + 1) * step]
        from_left = lax.ppermute(mine, "tensor", right)
        from_right = lax.ppermute(mine, "tensor", left)
        outer = jnp.where(t < 2, from_left, from_right)
        inner = jnp.where(t < 2, from_right, from_left)
        distant = lax.ppermute(outer, "tensor", swap)
        helped = dot(inner, help_weight[:depth]) + dot(distant, help_weight[depth:])
        helped = lax.ppermute(helped.astype(jnp.bfloat16), "tensor", [(1, 0), (2, 3)])
        total = dot(mine, own_w) + dot(from_left, left_w) + dot(from_right, right_w)
        total = total + dot(distant, distant_w) + delta[c * step : (c + 1) * step]
        outs.append((total + helped.astype(jnp.float32)).astype(jnp.bfloat16))
    return jnp.concatenate(outs, axis=0)


def solution(mesh):
    placed = (
        P(("groups", "replica"), "tensor"),
        P(None, "tensor"),
        P("replica", "tensor", None),
        P("replica", None, "tensor"),
        P("groups", None, None),
        P(("groups", "replica")),
        P(("groups", "replica")),
    )
    peers = mesh.shape["groups"] * mesh.shape["replica"]
    body = shards_line4 if mesh.shape["tensor"] == 4 and peers % 2 == 0 else shards_any
    return jax.shard_map(
        body,
        mesh=mesh,
        in_specs=placed,
        out_specs=P(("groups", "replica"), "tensor"),
        check_vma=False,
    )
```

```python
import jax
import jax.numpy as jnp
from jax import lax
from jax.experimental import pallas as pl
from jax.experimental.pallas import tpu as pltpu
from jax.sharding import PartitionSpec as P

CHUNKS = 4
TILE = 256
MESH = pl.DeviceIdType.MESH

DOWN, UP, PIECE = 0, 3, 6
ALONG_X, ALONG_Y, MATE = 7, 8, 9
X_THEN_Y, Y_THEN_X = 10, 11
MATE_X, MATE_Y, MATE_D0, MATE_D1 = 12, 13, 14, 15
NEAR_END, NEAR_MID, SHRINK = 16, 17, 18
OUTER, FORWARD, HELPED = 21, 21 + CHUNKS, 21 + 2 * CHUNKS
COPIES = 21 + 3 * CHUNKS


def exchange_adapters(adapter_down, adapter_up, send_table):
    me = lax.axis_index("replica")
    count = lax.axis_size("replica")
    downs, ups = [], []
    for k in range(count):
        wanted = send_table[me, me ^ k]
        down = adapter_down[wanted]
        up = adapter_up[wanted]
        if k:
            perm = [(i, i ^ k) for i in range(count)]
            down = lax.ppermute(down, "replica", perm)
            up = lax.ppermute(up, "replica", perm)
        downs.append(down)
        ups.append(up)
    return downs, ups


def adapter_term(tokens, adapter_down, adapter_up, send_table, block_slot, live_block_rows):
    count = live_block_rows.shape[0]
    block_rows = tokens.shape[0] // count
    slots_each = send_table.shape[2]
    rank = adapter_down.shape[2]
    me = lax.axis_index("replica")
    downs, ups = exchange_adapters(adapter_down, adapter_up, send_table)
    place = ((block_slot // slots_each) ^ me) * slots_each + block_slot % slots_each
    row_place = jnp.repeat(place, block_rows)
    partial = jnp.zeros((tokens.shape[0], rank), jnp.float32)
    for k, down in enumerate(downs):
        product = jnp.einsum("rd,cdx->rcx", tokens, down, preferred_element_type=jnp.float32)
        for c in range(slots_each):
            partial = jnp.where((row_place == k * slots_each + c)[:, None], product[:, c], partial)
    shrink_round = lax.psum(partial, "tensor").astype(jnp.bfloat16)
    live = jnp.arange(block_rows, dtype=jnp.int32)[None, :] < live_block_rows[:, None]
    live = live.reshape(-1)
    pieces = len(downs) * slots_each
    spread = jnp.where(
        (live[:, None] & (row_place[:, None] == jnp.arange(pieces, dtype=jnp.int32)[None, :]))[:, :, None],
        shrink_round[:, None, :],
        jnp.bfloat16(0),
    ).reshape(tokens.shape[0], pieces * rank)
    up_all = jnp.concatenate(ups, axis=0).reshape(pieces * rank, -1)
    return jnp.dot(spread, up_all, preferred_element_type=jnp.float32)


def shards_any(tokens, query_weight, adapter_down, adapter_up, send_table, block_slot, live_block_rows):
    delta = adapter_term(tokens, adapter_down, adapter_up, send_table, block_slot, live_block_rows)
    base = jnp.dot(
        lax.all_gather(tokens, "tensor", axis=1, tiled=True),
        query_weight,
        preferred_element_type=jnp.float32,
    )
    return (base + delta).astype(jnp.bfloat16)


def line4_kernel(
    tokens, weight, down_send, up_send, code, out,
    w, help_w, own, near, outer, distant, acc, acc_h, h_send, h_recv, downs, ups, spread, shr,
    send, recv, local,
):
    g, r, t = lax.axis_index("groups"), lax.axis_index("replica"), lax.axis_index("tensor")
    rows, depth = own.shape
    step = rows // CHUNKS
    each = help_w.shape[0] // 8
    is_end = (t == 0) | (t == 3)
    is_mid = (t == 1) | (t == 2)
    inner = jnp.where(t < 2, t + 1, t - 1)
    edge = jnp.where(t < 2, 0, 3)
    other = 3 - t
    near_at = jnp.where(t < 2, 2, 1)
    far_at = jnp.where(t < 2, 3, 0)
    inner_at = jnp.where(is_end, inner, other)

    def remote(i, src, dst, **device_id):
        return pltpu.make_async_remote_copy(
            src_ref=src, dst_ref=dst, send_sem=send.at[i], recv_sem=recv.at[i],
            device_id=device_id, device_id_type=MESH,
        )

    def block(i):
        return pl.ds(pl.multiple_of(i * depth, depth), depth)

    def part(c):
        return pl.ds(c * step, step)

    def load_w(n, i):
        return pltpu.make_async_copy(weight.at[block(i)], w.at[block(i)], local.at[n])

    local_own = pltpu.make_async_copy(tokens, own, local.at[4])
    local_down = pltpu.make_async_copy(down_send.at[0], downs.at[0], local.at[5])
    local_up = pltpu.make_async_copy(up_send.at[0], ups.at[0], local.at[6])
    local_own.start()
    loads = [load_w(n, lax.rem(t + n, 4)) for n in range(4)]
    loads[0].start()

    barrier = pltpu.get_barrier_semaphore()
    for d in range(1, 4):
        pl.semaphore_signal(barrier, inc=1, device_id={"tensor": lax.rem(t + d, 4)}, device_id_type=MESH)
        pl.semaphore_signal(barrier, inc=1, device_id={"replica": r ^ d}, device_id_type=MESH)
    pl.semaphore_signal(barrier, inc=1, device_id={"groups": 1 - g}, device_id_type=MESH)
    pl.semaphore_wait(barrier, 7)

    peer = g * 4 + r

    def spot(p, half=None):
        if half is None:
            return help_w.at[pl.ds(pl.multiple_of(p * each, each), each)]
        return help_w.at[pl.ds(pl.multiple_of(p * each + half * (each // 2), each // 2), each // 2)]

    rx, gy, rc = r ^ 2, 1 - g, r ^ 1
    px, py, pd = g * 4 + rx, gy * 4 + r, gy * 4 + rx
    piece_row = jnp.where(g == 0, near_at, far_at) * depth + r * each
    piece = remote(
        PIECE, weight.at[pl.ds(pl.multiple_of(piece_row, each), each)], spot(peer), tensor=inner
    )
    along_x = remote(ALONG_X, spot(peer), spot(peer), replica=rx)
    along_y = remote(ALONG_Y, spot(peer), spot(peer), groups=gy)
    mate = remote(MATE, spot(peer), spot(peer), replica=rc)
    x_then_y = remote(X_THEN_Y, spot(px, 0), spot(px, 0), groups=gy)
    y_then_x = remote(Y_THEN_X, spot(py, 1), spot(py, 1), replica=rx)
    mate_x = remote(MATE_X, spot(px), spot(px), replica=rc)
    mate_y = remote(MATE_Y, spot(py), spot(py), replica=rc)
    mate_d0 = remote(MATE_D0, spot(pd, 0), spot(pd, 0), replica=rc)
    mate_d1 = remote(MATE_D1, spot(pd, 1), spot(pd, 1), replica=rc)
    near_end = remote(NEAR_END, tokens, near, tensor=edge)
    near_mid = remote(NEAR_MID, tokens, near, tensor=other)
    to_inner = [remote(OUTER + c, tokens.at[part(c)], outer.at[part(c)], tensor=inner) for c in range(CHUNKS)]
    forward = [remote(FORWARD + c, outer.at[part(c)], distant.at[part(c)], tensor=other) for c in range(CHUNKS)]
    helped = [remote(HELPED + c, h_send.at[part(c)], h_recv.at[part(c)], tensor=edge) for c in range(CHUNKS)]
    adapters = []
    for k in (2, 3, 1):
        adapters.append(remote(DOWN + k - 1, down_send.at[k], downs.at[k], replica=r ^ k))
        adapters.append(remote(UP + k - 1, up_send.at[k], ups.at[k], replica=r ^ k))
    shrinks = [
        remote(SHRINK + d - 1, shr.at[t], shr.at[t], tensor=lax.rem(t + d, 4)) for d in range(1, 4)
    ]

    def product(x, x_rows, weights, w_rows, put):
        def tile(n, carry):
            cols = pl.ds(pl.multiple_of(n * TILE, TILE), TILE)
            put(cols, jnp.dot(x[x_rows, :], weights[w_rows, cols], preferred_element_type=jnp.float32))
            return carry

        lax.fori_loop(0, w.shape[1] // TILE, tile, 0)

    everything = pl.ds(0, rows)

    def add_base(x, x_rows, i):
        def put(cols, value):
            acc[x_rows, cols] += value

        product(x, x_rows, w, block(i), put)

    def own_base():
        local_own.wait()
        loads[0].wait()

        def put(cols, value):
            acc[:, cols] = value

        product(own, everything, w, block(t), put)

    low = lax.broadcasted_iota(jnp.int32, (rows, 128), 1) < 64

    def shrink_send():
        for copy in adapters:
            copy.wait_recv()
        local_down.wait()
        total = jnp.zeros((rows, 128), jnp.float32)
        for k in range(4):
            value = jnp.dot(own[...], downs[k], preferred_element_type=jnp.float32)
            hit = code[...] == jnp.where(low, 2 * k, 2 * k + 1)
            total = total + jnp.where(hit, value, 0.0)
        both = total + pltpu.roll(total, 64, 1)
        half = rows // 2
        shr[t] = jnp.where(low[:half], both[:half], both[half:])
        for copy in shrinks:
            copy.start()

    def add_delta():
        for d in range(1, 4):
            from_t = lax.rem(t + 4 - d, 4)
            remote(SHRINK + d - 1, shr.at[from_t], shr.at[from_t], tensor=lax.rem(t + d, 4)).wait_recv()
        local_up.wait()
        total = (shr[0] + shr[1]) + (shr[2] + shr[3])
        turned = pltpu.roll(total, 64, 1)
        half = rows // 2
        top = low[:half]
        both = jnp.concatenate([jnp.where(top, total, turned), jnp.where(top, turned, total)], axis=0)
        for k in range(4):
            hit = code[...] == jnp.where(low, 2 * k, 2 * k + 1)
            spread[:, k * 128 : (k + 1) * 128] = jnp.where(hit, both, 0.0).astype(jnp.bfloat16)

        def tile(n, carry):
            cols = pl.ds(pl.multiple_of(n * TILE, TILE), TILE)
            value = jnp.zeros((rows, TILE), jnp.float32)
            for k in range(4):
                value = value + jnp.dot(
                    spread[:, k * 128 : (k + 1) * 128], ups[k, :, cols], preferred_element_type=jnp.float32
                )
            acc[:, cols] += value
            return carry

        lax.fori_loop(0, w.shape[1] // TILE, tile, 0)

    @pl.when(is_end)
    def _():
        piece.start()

    @pl.when(is_mid)
    def _():
        near_mid.start()
        near_end.start()

    for copy in adapters:
        copy.start()
    local_down.start()
    local_up.start()
    for load in loads[1:]:
        load.start()
    own_base()
    for load in loads[1:]:
        load.wait()

    @pl.when(is_end)
    def _():
        piece.wait_send()
        to_inner[0].start()
        to_inner[1].start()
        to_inner[0].wait_send()
        to_inner[2].start()
        to_inner[1].wait_send()
        to_inner[3].start()
        shrink_send()
        near_end.wait_recv()
        add_base(near, everything, inner_at)
        add_delta()
        for c in range(CHUNKS):
            helped[c].wait_recv()
            out[part(c), :] = (acc[part(c), :] + h_recv[part(c), :].astype(jnp.float32)).astype(out.dtype)
        to_inner[2].wait_send()
        to_inner[3].wait_send()

    @pl.when(is_mid)
    def _():
        piece.wait_recv()
        along_x.start()
        along_y.start()
        mate.start()
        to_inner[0].wait_recv()
        forward[0].start()
        remote(ALONG_X, spot(px), spot(px), replica=rx).wait_recv()
        x_then_y.start()
        mate_x.start()
        remote(ALONG_Y, spot(py), spot(py), groups=gy).wait_recv()
        y_then_x.start()
        mate_y.start()
        to_inner[1].wait_recv()
        forward[1].start()
        shrink_send()
        near_mid.wait_recv()
        add_base(near, everything, inner_at)
        to_inner[2].wait_recv()
        forward[2].start()
        remote(X_THEN_Y, spot(pd, 0), spot(pd, 0), groups=gy).wait_recv()
        mate_d0.start()
        remote(Y_THEN_X, spot(pd, 1), spot(pd, 1), replica=rx).wait_recv()
        mate_d1.start()
        to_inner[3].wait_recv()
        forward[3].start()
        add_base(outer, everything, edge)
        pc = g * 4 + rc
        remote(MATE, spot(pc), spot(pc), replica=rc).wait_recv()
        remote(MATE_X, spot(pc ^ 2), spot(pc ^ 2), replica=rc).wait_recv()
        remote(MATE_Y, spot(gy * 4 + rc), spot(gy * 4 + rc), replica=rc).wait_recv()
        qd = gy * 4 + (rc ^ 2)
        remote(MATE_D0, spot(qd, 0), spot(qd, 0), replica=rc).wait_recv()
        remote(MATE_D1, spot(qd, 1), spot(qd, 1), replica=rc).wait_recv()

        def put_near(cols, value):
            acc_h[:, cols] = value

        product(near, everything, help_w, pl.ds(0, depth), put_near)
        add_delta()
        for c in range(CHUNKS):
            forward[c].wait_recv()

            def put_far(cols, value):
                h_send[part(c), cols] = (acc_h[part(c), cols] + value).astype(jnp.bfloat16)

            product(distant, part(c), help_w, pl.ds(depth, depth), put_far)
            helped[c].start()
            add_base(distant, part(c), 3 - edge)
            out[part(c), :] = acc[part(c), :].astype(out.dtype)
        for copy in [near_mid, near_end, along_x, along_y, mate, x_then_y, y_then_x]:
            copy.wait_send()
        for copy in [mate_x, mate_y, mate_d0, mate_d1] + forward + helped:
            copy.wait_send()

    for copy in adapters + shrinks:
        copy.wait_send()


def shards_line4(tokens, query_weight, adapter_down, adapter_up, send_table, block_slot, live_block_rows):
    me = lax.axis_index("replica")
    rows, depth = tokens.shape
    cols = query_weight.shape[1]
    rank = adapter_down.shape[2]
    wanted = jnp.concatenate([send_table[me, me ^ k] for k in range(4)])
    down_send = adapter_down[wanted].reshape(4, 2, depth, rank).transpose(0, 2, 1, 3).reshape(4, depth, 2 * rank)
    up_send = adapter_up[wanted].reshape(4, 2 * rank, cols)
    count = block_slot.shape[0]
    place = ((block_slot // 2) ^ me) * 2 + block_slot % 2
    live = jnp.arange(rows // count, dtype=jnp.int32)[None, :] < live_block_rows[:, None]
    code = jnp.where(live, place[:, None], -1).reshape(rows, 1)
    code = jnp.broadcast_to(code, (rows, 128))
    bf16, f32 = jnp.bfloat16, jnp.float32
    any_space = pl.BlockSpec(memory_space=pl.ANY)
    vmem = pl.BlockSpec(memory_space=pltpu.VMEM)
    return pl.pallas_call(
        line4_kernel,
        out_shape=jax.ShapeDtypeStruct((rows, cols), bf16),
        in_specs=[any_space] * 4 + [vmem],
        out_specs=vmem,
        scratch_shapes=[
            pltpu.VMEM((4 * depth, cols), bf16),
            pltpu.VMEM((2 * depth, cols), bf16),
            pltpu.VMEM((rows, depth), bf16),
            pltpu.VMEM((rows, depth), bf16),
            pltpu.VMEM((rows, depth), bf16),
            pltpu.VMEM((rows, depth), bf16),
            pltpu.VMEM((rows, cols), f32),
            pltpu.VMEM((rows, cols), f32),
            pltpu.VMEM((rows, cols), bf16),
            pltpu.VMEM((rows, cols), bf16),
            pltpu.VMEM((4, depth, 2 * rank), bf16),
            pltpu.VMEM((4, 2 * rank, cols), bf16),
            pltpu.VMEM((rows, 8 * rank), bf16),
            pltpu.VMEM((4, rows // 2, 128), f32),
            pltpu.SemaphoreType.DMA((COPIES,)),
            pltpu.SemaphoreType.DMA((COPIES,)),
            pltpu.SemaphoreType.DMA((7,)),
        ],
        compiler_params=pltpu.CompilerParams(
            collective_id=0, has_side_effects=True, vmem_limit_bytes=56 << 20
        ),
        cost_estimate=pl.CostEstimate(flops=13 * 10**9, bytes_accessed=40 << 20, transcendentals=0),
    )(tokens, query_weight, down_send, up_send, code)


def solution(mesh):
    placed = (
        P(("groups", "replica"), "tensor"),
        P(None, "tensor"),
        P("replica", "tensor", None),
        P("replica", None, "tensor"),
        P("groups", None, None),
        P(("groups", "replica")),
        P(("groups", "replica")),
    )
    sizes = (mesh.shape["groups"], mesh.shape["replica"], mesh.shape["tensor"])
    body = shards_line4 if sizes == (2, 4, 4) else shards_any
    return jax.shard_map(
        body,
        mesh=mesh,
        in_specs=placed,
        out_specs=P(("groups", "replica"), "tensor"),
        check_vma=False,
    )
```

```python
import jax
import jax.numpy as jnp
from jax import lax
from jax.experimental import pallas as pl
from jax.experimental.pallas import tpu as pltpu
from jax.sharding import PartitionSpec as P

CHUNKS = 8
TILE = 256
MESH = pl.DeviceIdType.MESH

DOWN, UP, PIECE = 0, 3, 6
ALONG_X, ALONG_Y, MATE = 8, 10, 12
X_THEN_Y, Y_THEN_X = 13, 14
MATE_X, MATE_Y, MATE_D0, MATE_D1 = 15, 16, 17, 18
NEAR_END, NEAR_MID, SHRINK = 19, 20, 21
OUTER, FORWARD, HELPED = 24, 24 + CHUNKS, 24 + 2 * CHUNKS
COPIES = 24 + 3 * CHUNKS


def exchange_adapters(adapter_down, adapter_up, send_table):
    me = lax.axis_index("replica")
    count = lax.axis_size("replica")
    downs, ups = [], []
    for k in range(count):
        wanted = send_table[me, me ^ k]
        down = adapter_down[wanted]
        up = adapter_up[wanted]
        if k:
            perm = [(i, i ^ k) for i in range(count)]
            down = lax.ppermute(down, "replica", perm)
            up = lax.ppermute(up, "replica", perm)
        downs.append(down)
        ups.append(up)
    return downs, ups


def adapter_term(tokens, adapter_down, adapter_up, send_table, block_slot, live_block_rows):
    count = live_block_rows.shape[0]
    block_rows = tokens.shape[0] // count
    slots_each = send_table.shape[2]
    rank = adapter_down.shape[2]
    me = lax.axis_index("replica")
    downs, ups = exchange_adapters(adapter_down, adapter_up, send_table)
    place = ((block_slot // slots_each) ^ me) * slots_each + block_slot % slots_each
    row_place = jnp.repeat(place, block_rows)
    partial = jnp.zeros((tokens.shape[0], rank), jnp.float32)
    for k, down in enumerate(downs):
        product = jnp.einsum("rd,cdx->rcx", tokens, down, preferred_element_type=jnp.float32)
        for c in range(slots_each):
            partial = jnp.where((row_place == k * slots_each + c)[:, None], product[:, c], partial)
    shrink_round = lax.psum(partial, "tensor").astype(jnp.bfloat16)
    live = jnp.arange(block_rows, dtype=jnp.int32)[None, :] < live_block_rows[:, None]
    live = live.reshape(-1)
    pieces = len(downs) * slots_each
    spread = jnp.where(
        (live[:, None] & (row_place[:, None] == jnp.arange(pieces, dtype=jnp.int32)[None, :]))[:, :, None],
        shrink_round[:, None, :],
        jnp.bfloat16(0),
    ).reshape(tokens.shape[0], pieces * rank)
    up_all = jnp.concatenate(ups, axis=0).reshape(pieces * rank, -1)
    return jnp.dot(spread, up_all, preferred_element_type=jnp.float32)


def shards_any(tokens, query_weight, adapter_down, adapter_up, send_table, block_slot, live_block_rows):
    delta = adapter_term(tokens, adapter_down, adapter_up, send_table, block_slot, live_block_rows)
    base = jnp.dot(
        lax.all_gather(tokens, "tensor", axis=1, tiled=True),
        query_weight,
        preferred_element_type=jnp.float32,
    )
    return (base + delta).astype(jnp.bfloat16)


def line4_kernel(
    tokens, weight, adapter_down, adapter_up, send_table, block_slot, live_rows, out,
    w, help_w, own, near, outer, distant, acc, acc_h, h_send, h_recv, downs, ups, spread, shr,
    code, down_all, up_all, down_send, up_send, send, recv, local,
):
    g, r, t = lax.axis_index("groups"), lax.axis_index("replica"), lax.axis_index("tensor")
    rows, depth = own.shape
    step = rows // CHUNKS
    each = help_w.shape[0] // 8
    is_end = (t == 0) | (t == 3)
    is_mid = (t == 1) | (t == 2)
    inner = jnp.where(t < 2, t + 1, t - 1)
    edge = jnp.where(t < 2, 0, 3)
    other = 3 - t
    near_at = jnp.where(t < 2, 2, 1)
    far_at = jnp.where(t < 2, 3, 0)
    inner_at = jnp.where(is_end, inner, other)

    def remote(i, src, dst, **device_id):
        return pltpu.make_async_remote_copy(
            src_ref=src, dst_ref=dst, send_sem=send.at[i], recv_sem=recv.at[i],
            device_id=device_id, device_id_type=MESH,
        )

    def block(i):
        return pl.ds(pl.multiple_of(i * depth, depth), depth)

    def part(c):
        return pl.ds(c * step, step)

    def load_w(n, i):
        return pltpu.make_async_copy(weight.at[block(i)], w.at[block(i)], local.at[n])

    local_own = pltpu.make_async_copy(tokens, own, local.at[4])
    local_down = pltpu.make_async_copy(adapter_down, down_all, local.at[5])
    local_up = pltpu.make_async_copy(adapter_up, up_all, local.at[6])
    local_down.start()
    local_up.start()
    local_own.start()
    loads = [load_w(n, lax.rem(t + n, 4)) for n in range(4)]
    loads[0].start()

    barrier = pltpu.get_barrier_semaphore()
    for d in range(1, 4):
        pl.semaphore_signal(barrier, inc=1, device_id={"tensor": lax.rem(t + d, 4)}, device_id_type=MESH)
        pl.semaphore_signal(barrier, inc=1, device_id={"replica": r ^ d}, device_id_type=MESH)
    pl.semaphore_signal(barrier, inc=1, device_id={"groups": 1 - g}, device_id_type=MESH)
    pl.semaphore_wait(barrier, 7)

    peer = g * 4 + r

    def spot(p, half=None):
        if half is None:
            return help_w.at[pl.ds(pl.multiple_of(p * each, each), each)]
        return help_w.at[pl.ds(pl.multiple_of(p * each + half * (each // 2), each // 2), each // 2)]

    rx, gy, rc = r ^ 2, 1 - g, r ^ 1
    px, py, pd = g * 4 + rx, gy * 4 + r, gy * 4 + rx
    piece_row = jnp.where(g == 0, near_at, far_at) * depth + r * each
    half_piece = each // 2
    pieces = [
        remote(
            PIECE + h,
            weight.at[pl.ds(pl.multiple_of(piece_row + h * half_piece, half_piece), half_piece)],
            spot(peer, h),
            tensor=inner,
        )
        for h in range(2)
    ]
    along_x = [remote(ALONG_X + h, spot(peer, h), spot(peer, h), replica=rx) for h in range(2)]
    along_y = [remote(ALONG_Y + h, spot(peer, h), spot(peer, h), groups=gy) for h in range(2)]
    from_x = [remote(ALONG_X + h, spot(px, h), spot(px, h), replica=rx) for h in range(2)]
    from_y = [remote(ALONG_Y + h, spot(py, h), spot(py, h), groups=gy) for h in range(2)]
    mate = remote(MATE, spot(peer), spot(peer), replica=rc)
    x_then_y = remote(X_THEN_Y, spot(px, 0), spot(px, 0), groups=gy)
    y_then_x = remote(Y_THEN_X, spot(py, 1), spot(py, 1), replica=rx)
    mate_x = remote(MATE_X, spot(px), spot(px), replica=rc)
    mate_y = remote(MATE_Y, spot(py), spot(py), replica=rc)
    mate_d0 = remote(MATE_D0, spot(pd, 0), spot(pd, 0), replica=rc)
    mate_d1 = remote(MATE_D1, spot(pd, 1), spot(pd, 1), replica=rc)
    near_end = remote(NEAR_END, tokens, near, tensor=edge)
    near_mid = remote(NEAR_MID, tokens, near, tensor=other)
    to_inner = [remote(OUTER + c, tokens.at[part(c)], outer.at[part(c)], tensor=inner) for c in range(CHUNKS)]
    forward = [remote(FORWARD + c, outer.at[part(c)], distant.at[part(c)], tensor=other) for c in range(CHUNKS)]
    helped = [remote(HELPED + c, h_send.at[part(c)], h_recv.at[part(c)], tensor=edge) for c in range(CHUNKS)]
    adapters = []
    for k in (2, 3, 1):
        adapters.append(remote(DOWN + k - 1, down_send.at[k - 1], downs.at[k], replica=r ^ k))
        adapters.append(remote(UP + k - 1, up_send.at[k - 1], ups.at[k], replica=r ^ k))
    shrink_in = remote(SHRINK, shr.at[0], shr.at[1], tensor=inner)
    shrink_mid = remote(SHRINK + 1, shr.at[2], shr.at[3], tensor=other)
    shrink_out = remote(SHRINK + 2, shr.at[4], shr.at[4], tensor=edge)

    def product(x, x_rows, weights, w_rows, put):
        def tile(n, carry):
            cols = pl.ds(pl.multiple_of(n * TILE, TILE), TILE)
            put(cols, jnp.dot(x[x_rows, :], weights[w_rows, cols], preferred_element_type=jnp.float32))
            return carry

        lax.fori_loop(0, w.shape[1] // TILE, tile, 0)

    everything = pl.ds(0, rows)

    def add_base(x, x_rows, i):
        def put(cols, value):
            acc[x_rows, cols] += value

        product(x, x_rows, w, block(i), put)

    def own_base():
        local_own.wait()
        loads[0].wait()

        def put(cols, value):
            acc[:, cols] = value

        product(own, everything, w, block(t), put)

    low = lax.broadcasted_iota(jnp.int32, (rows, 128), 1) < 64

    def pick_adapters():
        local_down.wait()
        local_up.wait()
        for k in range(4):
            for c in range(2):
                wanted = send_table[r, r ^ k, c]
                down, up = down_all[wanted], up_all[wanted]
                if k:
                    down_send[k - 1, c * 64 : (c + 1) * 64] = down
                    up_send[k - 1, c * 64 : (c + 1) * 64] = up
                else:
                    downs[0, c * 64 : (c + 1) * 64] = down
                    ups[0, c * 64 : (c + 1) * 64] = up
        for copy in adapters:
            copy.start()

    def write_codes():
        count = block_slot.shape[0]
        size = rows // count
        row = lax.broadcasted_iota(jnp.int32, (size, 128), 0)
        for b in range(count):
            slot = block_slot[b]
            place = ((slot >> 1) ^ r) * 2 + (slot & 1)
            code[b * size : (b + 1) * size, :] = jnp.where(row < live_rows[b], place, -1)

    def partial_shrink():
        for copy in adapters:
            copy.wait_recv()
        total = jnp.zeros((rows, 128), jnp.float32)
        for k in range(4):
            value = lax.dot_general(
                own[...], downs[k], (((1,), (1,)), ((), ())), preferred_element_type=jnp.float32
            )
            hit = code[...] == jnp.where(low, 2 * k, 2 * k + 1)
            total = total + jnp.where(hit, value, 0.0)
        both = total + pltpu.roll(total, 64, 1)
        half = rows // 2
        shr[0] = jnp.where(low[:half], both[:half], both[half:])

    def add_delta():
        total = shr[4]
        turned = pltpu.roll(total, 64, 1)
        half = rows // 2
        top = low[:half]
        both = jnp.concatenate([jnp.where(top, total, turned), jnp.where(top, turned, total)], axis=0)
        for k in range(4):
            hit = code[...] == jnp.where(low, 2 * k, 2 * k + 1)
            spread[:, k * 128 : (k + 1) * 128] = jnp.where(hit, both, 0.0).astype(jnp.bfloat16)

        def tile(n, carry):
            cols = pl.ds(pl.multiple_of(n * TILE, TILE), TILE)
            value = jnp.zeros((rows, TILE), jnp.float32)
            for k in range(4):
                value = value + jnp.dot(
                    spread[:, k * 128 : (k + 1) * 128], ups[k, :, cols], preferred_element_type=jnp.float32
                )
            acc[:, cols] += value
            return carry

        lax.fori_loop(0, w.shape[1] // TILE, tile, 0)

    @pl.when(is_end)
    def _():
        pieces[0].start()
        pieces[1].start()

    @pl.when(is_mid)
    def _():
        near_mid.start()
        near_end.start()

    pick_adapters()
    for load in loads[1:]:
        load.start()
    write_codes()
    own_base()
    for load in loads[1:]:
        load.wait()

    @pl.when(is_end)
    def _():
        def follow(c):
            to_inner[c - 2].wait_send()
            to_inner[c].start()

        pieces[0].wait_send()
        to_inner[0].start()
        pieces[1].wait_send()
        to_inner[1].start()
        for c in range(2, CHUNKS - 2):
            follow(c)
        partial_shrink()
        shrink_in.start()
        for c in range(CHUNKS - 2, CHUNKS):
            follow(c)
        near_end.wait_recv()
        add_base(near, everything, inner_at)
        shrink_out.wait_recv()
        add_delta()
        for c in range(CHUNKS):
            helped[c].wait_recv()
            out[part(c), :] = (acc[part(c), :] + h_recv[part(c), :].astype(jnp.float32)).astype(out.dtype)
        to_inner[CHUNKS - 2].wait_send()
        to_inner[CHUNKS - 1].wait_send()
        shrink_in.wait_send()

    @pl.when(is_mid)
    def _():
        def relay(*chunks):
            for c in chunks:
                to_inner[c].wait_recv()
                forward[c].start()

        for h in range(2):
            pieces[h].wait_recv()
            along_x[h].start()
            along_y[h].start()
        mate.start()
        from_x[0].wait_recv()
        x_then_y.start()
        relay(0, 1)
        from_y[0].wait_recv()
        from_y[1].wait_recv()
        y_then_x.start()
        mate_y.start()
        relay(2)
        from_x[1].wait_recv()
        mate_x.start()
        relay(3)
        partial_shrink()
        near_mid.wait_recv()
        add_base(near, everything, inner_at)
        relay(4)
        remote(X_THEN_Y, spot(pd, 0), spot(pd, 0), groups=gy).wait_recv()
        mate_d0.start()
        remote(Y_THEN_X, spot(pd, 1), spot(pd, 1), replica=rx).wait_recv()
        mate_d1.start()
        relay(5)
        shrink_in.wait_recv()
        shr[2] = shr[0] + shr[1]
        shrink_mid.start()
        relay(6)
        pc = g * 4 + rc
        remote(MATE, spot(pc), spot(pc), replica=rc).wait_recv()
        remote(MATE_X, spot(pc ^ 2), spot(pc ^ 2), replica=rc).wait_recv()
        remote(MATE_Y, spot(gy * 4 + rc), spot(gy * 4 + rc), replica=rc).wait_recv()
        qd = gy * 4 + (rc ^ 2)
        remote(MATE_D0, spot(qd, 0), spot(qd, 0), replica=rc).wait_recv()
        remote(MATE_D1, spot(qd, 1), spot(qd, 1), replica=rc).wait_recv()
        relay(7)

        def put_near(cols, value):
            acc_h[:, cols] = value

        product(near, everything, help_w, pl.ds(0, depth), put_near)
        shrink_mid.wait_recv()
        shr[4] = shr[2] + shr[3]
        shrink_out.start()

        def help_edge(c):
            forward[c].wait_recv()

            def put_far(cols, value):
                h_send[part(c), cols] = (acc_h[part(c), cols] + value).astype(jnp.bfloat16)

            product(distant, part(c), help_w, pl.ds(depth, depth), put_far)
            helped[c].start()

        def finish(c):
            add_base(distant, part(c), 3 - edge)
            out[part(c), :] = acc[part(c), :].astype(out.dtype)

        help_edge(0)
        help_edge(1)
        add_base(outer, everything, edge)
        help_edge(2)
        add_delta()
        help_edge(3)
        for c in range(4):
            finish(c)
        for c in range(4, CHUNKS):
            help_edge(c)
            finish(c)
        for copy in [near_mid, near_end, mate, x_then_y, y_then_x, shrink_mid, shrink_out]:
            copy.wait_send()
        for copy in along_x + along_y + [mate_x, mate_y, mate_d0, mate_d1] + forward + helped:
            copy.wait_send()

    for copy in adapters:
        copy.wait_send()


def shards_line4(tokens, query_weight, adapter_down, adapter_up, send_table, block_slot, live_block_rows):
    rows, depth = tokens.shape
    cols = query_weight.shape[1]
    rank = adapter_down.shape[2]
    adapter_down = adapter_down.transpose(0, 2, 1)
    bf16, f32 = jnp.bfloat16, jnp.float32
    any_space = pl.BlockSpec(memory_space=pl.ANY)
    vmem = pl.BlockSpec(memory_space=pltpu.VMEM)
    smem = pl.BlockSpec(memory_space=pltpu.SMEM)
    return pl.pallas_call(
        line4_kernel,
        out_shape=jax.ShapeDtypeStruct((rows, cols), bf16),
        in_specs=[any_space] * 4 + [smem] * 3,
        out_specs=vmem,
        scratch_shapes=[
            pltpu.VMEM((4 * depth, cols), bf16),
            pltpu.VMEM((2 * depth, cols), bf16),
            pltpu.VMEM((rows, depth), bf16),
            pltpu.VMEM((rows, depth), bf16),
            pltpu.VMEM((rows, depth), bf16),
            pltpu.VMEM((rows, depth), bf16),
            pltpu.VMEM((rows, cols), f32),
            pltpu.VMEM((rows, cols), f32),
            pltpu.VMEM((rows, cols), bf16),
            pltpu.VMEM((rows, cols), bf16),
            pltpu.VMEM((4, 2 * rank, depth), bf16),
            pltpu.VMEM((4, 2 * rank, cols), bf16),
            pltpu.VMEM((rows, 8 * rank), bf16),
            pltpu.VMEM((5, rows // 2, 128), f32),
            pltpu.VMEM((rows, 128), jnp.int32),
            pltpu.VMEM(adapter_down.shape, bf16),
            pltpu.VMEM(adapter_up.shape, bf16),
            pltpu.VMEM((3, 2 * rank, depth), bf16),
            pltpu.VMEM((3, 2 * rank, cols), bf16),
            pltpu.SemaphoreType.DMA((COPIES,)),
            pltpu.SemaphoreType.DMA((COPIES,)),
            pltpu.SemaphoreType.DMA((7,)),
        ],
        compiler_params=pltpu.CompilerParams(
            collective_id=0, has_side_effects=True, vmem_limit_bytes=60 << 20
        ),
        cost_estimate=pl.CostEstimate(flops=13 * 10**9, bytes_accessed=40 << 20, transcendentals=0),
    )(tokens, query_weight, adapter_down, adapter_up, send_table, block_slot, live_block_rows)


def solution(mesh):
    placed = (
        P(("groups", "replica"), "tensor"),
        P(None, "tensor"),
        P("replica", "tensor", None),
        P("replica", None, "tensor"),
        P("groups", None, None),
        P(("groups", "replica")),
        P(("groups", "replica")),
    )
    sizes = (mesh.shape["groups"], mesh.shape["replica"], mesh.shape["tensor"])
    body = shards_line4 if sizes == (2, 4, 4) else shards_any
    return jax.shard_map(
        body,
        mesh=mesh,
        in_specs=placed,
        out_specs=P(("groups", "replica"), "tensor"),
        check_vma=False,
    )
```

```python
import jax
import jax.numpy as jnp
from jax import lax
from jax.experimental import pallas as pl
from jax.experimental.pallas import tpu as pltpu
from jax.sharding import PartitionSpec as P

CHUNKS = 8
TILE = 256
GROUPS = ((0, 4), (4, 2), (6, 1), (7, 1))
MESH = pl.DeviceIdType.MESH

DOWN, UP, PIECE = 0, 3, 6
ALONG_X, ALONG_Y, MATE = 8, 10, 12
X_THEN_Y, Y_THEN_X = 13, 14
MATE_X, MATE_Y, MATE_D0, MATE_D1 = 15, 16, 17, 18
NEAR_END, NEAR_MID, SHRINK = 19, 20, 21
OUTER, FORWARD, HELPED = 24, 24 + CHUNKS, 24 + 2 * CHUNKS
COPIES = 24 + 3 * CHUNKS


def exchange_adapters(adapter_down, adapter_up, send_table):
    me = lax.axis_index("replica")
    count = lax.axis_size("replica")
    downs, ups = [], []
    for k in range(count):
        wanted = send_table[me, me ^ k]
        down = adapter_down[wanted]
        up = adapter_up[wanted]
        if k:
            perm = [(i, i ^ k) for i in range(count)]
            down = lax.ppermute(down, "replica", perm)
            up = lax.ppermute(up, "replica", perm)
        downs.append(down)
        ups.append(up)
    return downs, ups


def adapter_term(tokens, adapter_down, adapter_up, send_table, block_slot, live_block_rows):
    count = live_block_rows.shape[0]
    block_rows = tokens.shape[0] // count
    slots_each = send_table.shape[2]
    rank = adapter_down.shape[2]
    me = lax.axis_index("replica")
    downs, ups = exchange_adapters(adapter_down, adapter_up, send_table)
    place = ((block_slot // slots_each) ^ me) * slots_each + block_slot % slots_each
    row_place = jnp.repeat(place, block_rows)
    partial = jnp.zeros((tokens.shape[0], rank), jnp.float32)
    for k, down in enumerate(downs):
        product = jnp.einsum("rd,cdx->rcx", tokens, down, preferred_element_type=jnp.float32)
        for c in range(slots_each):
            partial = jnp.where((row_place == k * slots_each + c)[:, None], product[:, c], partial)
    shrink_round = lax.psum(partial, "tensor").astype(jnp.bfloat16)
    live = jnp.arange(block_rows, dtype=jnp.int32)[None, :] < live_block_rows[:, None]
    live = live.reshape(-1)
    pieces = len(downs) * slots_each
    spread = jnp.where(
        (live[:, None] & (row_place[:, None] == jnp.arange(pieces, dtype=jnp.int32)[None, :]))[:, :, None],
        shrink_round[:, None, :],
        jnp.bfloat16(0),
    ).reshape(tokens.shape[0], pieces * rank)
    up_all = jnp.concatenate(ups, axis=0).reshape(pieces * rank, -1)
    return jnp.dot(spread, up_all, preferred_element_type=jnp.float32)


def shards_any(tokens, query_weight, adapter_down, adapter_up, send_table, block_slot, live_block_rows):
    delta = adapter_term(tokens, adapter_down, adapter_up, send_table, block_slot, live_block_rows)
    base = jnp.dot(
        lax.all_gather(tokens, "tensor", axis=1, tiled=True),
        query_weight,
        preferred_element_type=jnp.float32,
    )
    return (base + delta).astype(jnp.bfloat16)


def line4_kernel(
    tokens, weight, adapter_down, adapter_up, send_table, block_slot, live_rows, out,
    w, help_w, own, near, outer, distant, acc, acc_h, h_send, h_recv, downs, ups, spread, shr,
    code, down_all, up_all, down_send, up_send, send, recv, local,
):
    g, r, t = lax.axis_index("groups"), lax.axis_index("replica"), lax.axis_index("tensor")
    rows, depth = own.shape
    step = rows // CHUNKS
    each = help_w.shape[0] // 8
    is_end = (t == 0) | (t == 3)
    is_mid = (t == 1) | (t == 2)
    inner = jnp.where(t < 2, t + 1, t - 1)
    edge = jnp.where(t < 2, 0, 3)
    other = 3 - t
    near_at = jnp.where(t < 2, 2, 1)
    far_at = jnp.where(t < 2, 3, 0)
    inner_at = jnp.where(is_end, inner, other)

    def remote(i, src, dst, **device_id):
        return pltpu.make_async_remote_copy(
            src_ref=src, dst_ref=dst, send_sem=send.at[i], recv_sem=recv.at[i],
            device_id=device_id, device_id_type=MESH,
        )

    def block(i):
        return pl.ds(pl.multiple_of(i * depth, depth), depth)

    def part(c):
        return pl.ds(c * step, step)

    def load_w(n, i):
        return pltpu.make_async_copy(weight.at[block(i)], w.at[block(i)], local.at[n])

    local_own = pltpu.make_async_copy(tokens, own, local.at[4])
    local_down = pltpu.make_async_copy(adapter_down, down_all, local.at[5])
    local_up = pltpu.make_async_copy(adapter_up, up_all, local.at[6])
    local_down.start()
    local_up.start()
    local_own.start()
    loads = [load_w(n, lax.rem(t + n, 4)) for n in range(4)]
    loads[0].start()

    barrier = pltpu.get_barrier_semaphore()
    for d in range(1, 4):
        pl.semaphore_signal(barrier, inc=1, device_id={"tensor": lax.rem(t + d, 4)}, device_id_type=MESH)
        pl.semaphore_signal(barrier, inc=1, device_id={"replica": r ^ d}, device_id_type=MESH)
    pl.semaphore_signal(barrier, inc=1, device_id={"groups": 1 - g}, device_id_type=MESH)
    pl.semaphore_wait(barrier, 7)

    peer = g * 4 + r

    def spot(p, half=None):
        if half is None:
            return help_w.at[pl.ds(pl.multiple_of(p * each, each), each)]
        return help_w.at[pl.ds(pl.multiple_of(p * each + half * (each // 2), each // 2), each // 2)]

    rx, gy, rc = r ^ 2, 1 - g, r ^ 1
    px, py, pd = g * 4 + rx, gy * 4 + r, gy * 4 + rx
    piece_row = jnp.where(g == 0, near_at, far_at) * depth + r * each
    half_piece = each // 2
    pieces = [
        remote(
            PIECE + h,
            weight.at[pl.ds(pl.multiple_of(piece_row + h * half_piece, half_piece), half_piece)],
            spot(peer, h),
            tensor=inner,
        )
        for h in range(2)
    ]
    along_x = [remote(ALONG_X + h, spot(peer, h), spot(peer, h), replica=rx) for h in range(2)]
    along_y = [remote(ALONG_Y + h, spot(peer, h), spot(peer, h), groups=gy) for h in range(2)]
    from_x = [remote(ALONG_X + h, spot(px, h), spot(px, h), replica=rx) for h in range(2)]
    from_y = [remote(ALONG_Y + h, spot(py, h), spot(py, h), groups=gy) for h in range(2)]
    mate = remote(MATE, spot(peer), spot(peer), replica=rc)
    x_then_y = remote(X_THEN_Y, spot(px, 0), spot(px, 0), groups=gy)
    y_then_x = remote(Y_THEN_X, spot(py, 1), spot(py, 1), replica=rx)
    mate_x = remote(MATE_X, spot(px), spot(px), replica=rc)
    mate_y = remote(MATE_Y, spot(py), spot(py), replica=rc)
    mate_d0 = remote(MATE_D0, spot(pd, 0), spot(pd, 0), replica=rc)
    mate_d1 = remote(MATE_D1, spot(pd, 1), spot(pd, 1), replica=rc)
    near_end = remote(NEAR_END, tokens, near, tensor=edge)
    near_mid = remote(NEAR_MID, tokens, near, tensor=other)
    to_inner = [remote(OUTER + c, tokens.at[part(c)], outer.at[part(c)], tensor=inner) for c in range(CHUNKS)]
    forward = [remote(FORWARD + c, outer.at[part(c)], distant.at[part(c)], tensor=other) for c in range(CHUNKS)]
    group_rows = [pl.ds(c * step, n * step) for c, n in GROUPS]
    helped = [
        remote(HELPED + i, h_send.at[rows_of], h_recv.at[rows_of], tensor=edge)
        for i, rows_of in enumerate(group_rows)
    ]
    adapters = []
    for k in (2, 3, 1):
        adapters.append(remote(DOWN + k - 1, down_send.at[k - 1], downs.at[k], replica=r ^ k))
        adapters.append(remote(UP + k - 1, up_send.at[k - 1], ups.at[k], replica=r ^ k))
    shrink_in = remote(SHRINK, shr.at[0], shr.at[1], tensor=inner)
    shrink_mid = remote(SHRINK + 1, shr.at[2], shr.at[3], tensor=other)
    shrink_out = remote(SHRINK + 2, shr.at[4], shr.at[4], tensor=edge)

    def product(x, x_rows, weights, w_rows, put):
        def tile(n, carry):
            cols = pl.ds(pl.multiple_of(n * TILE, TILE), TILE)
            put(cols, jnp.dot(x[x_rows, :], weights[w_rows, cols], preferred_element_type=jnp.float32))
            return carry

        lax.fori_loop(0, w.shape[1] // TILE, tile, 0)

    everything = pl.ds(0, rows)

    def add_base(x, x_rows, i):
        def put(cols, value):
            acc[x_rows, cols] += value

        product(x, x_rows, w, block(i), put)

    def own_base():
        local_own.wait()
        loads[0].wait()

        def put(cols, value):
            acc[:, cols] = value

        product(own, everything, w, block(t), put)

    low = lax.broadcasted_iota(jnp.int32, (rows, 128), 1) < 64

    def pick_adapters():
        local_down.wait()
        local_up.wait()
        for k in range(4):
            for c in range(2):
                wanted = send_table[r, r ^ k, c]
                down, up = down_all[wanted], up_all[wanted]
                if k:
                    down_send[k - 1, c * 64 : (c + 1) * 64] = down
                    up_send[k - 1, c * 64 : (c + 1) * 64] = up
                else:
                    downs[0, c * 64 : (c + 1) * 64] = down
                    ups[0, c * 64 : (c + 1) * 64] = up
        adapters[0].start()
        adapters[4].start()
        adapters[5].start()

    def later_adapters():
        for copy in adapters[1:4]:
            copy.start()

    def write_codes():
        count = block_slot.shape[0]
        size = rows // count
        row = lax.broadcasted_iota(jnp.int32, (size, 128), 0)
        for b in range(count):
            slot = block_slot[b]
            place = ((slot >> 1) ^ r) * 2 + (slot & 1)
            code[b * size : (b + 1) * size, :] = jnp.where(row < live_rows[b], place, -1)

    def partial_shrink():
        for copy in adapters:
            copy.wait_recv()
        total = jnp.zeros((rows, 128), jnp.float32)
        for k in range(4):
            value = lax.dot_general(
                own[...], downs[k], (((1,), (1,)), ((), ())), preferred_element_type=jnp.float32
            )
            hit = code[...] == jnp.where(low, 2 * k, 2 * k + 1)
            total = total + jnp.where(hit, value, 0.0)
        both = total + pltpu.roll(total, 64, 1)
        half = rows // 2
        shr[0] = jnp.where(low[:half], both[:half], both[half:])

    def add_delta():
        total = shr[4]
        turned = pltpu.roll(total, 64, 1)
        half = rows // 2
        top = low[:half]
        both = jnp.concatenate([jnp.where(top, total, turned), jnp.where(top, turned, total)], axis=0)
        for k in range(4):
            hit = code[...] == jnp.where(low, 2 * k, 2 * k + 1)
            spread[:, k * 128 : (k + 1) * 128] = jnp.where(hit, both, 0.0).astype(jnp.bfloat16)

        def tile(n, carry):
            cols = pl.ds(pl.multiple_of(n * TILE, TILE), TILE)
            value = jnp.zeros((rows, TILE), jnp.float32)
            for k in range(4):
                value = value + jnp.dot(
                    spread[:, k * 128 : (k + 1) * 128], ups[k, :, cols], preferred_element_type=jnp.float32
                )
            acc[:, cols] += value
            return carry

        lax.fori_loop(0, w.shape[1] // TILE, tile, 0)

    @pl.when(is_end)
    def _():
        pieces[0].start()
        pieces[1].start()

    @pl.when(is_mid)
    def _():
        near_mid.start()
        near_end.start()

    pick_adapters()
    for load in loads[1:]:
        load.start()
    write_codes()
    own_base()
    for load in loads[1:]:
        load.wait()

    @pl.when(is_end)
    def _():
        def follow(c):
            to_inner[c - 2].wait_send()
            to_inner[c].start()

        later_adapters()
        pieces[0].wait_send()
        to_inner[0].start()
        pieces[1].wait_send()
        to_inner[1].start()
        for c in range(2, CHUNKS - 2):
            follow(c)
        partial_shrink()
        shrink_in.start()
        for c in range(CHUNKS - 2, CHUNKS):
            follow(c)
        near_end.wait_recv()
        add_base(near, everything, inner_at)
        shrink_out.wait_recv()
        add_delta()
        for copy, rows_of in zip(helped, group_rows):
            copy.wait_recv()
            out[rows_of, :] = (acc[rows_of, :] + h_recv[rows_of, :].astype(jnp.float32)).astype(out.dtype)
        to_inner[CHUNKS - 2].wait_send()
        to_inner[CHUNKS - 1].wait_send()
        shrink_in.wait_send()

    @pl.when(is_mid)
    def _():
        def relay(*chunks):
            for c in chunks:
                to_inner[c].wait_recv()
                forward[c].start()

        for h in range(2):
            pieces[h].wait_recv()
            along_x[h].start()
            along_y[h].start()
        mate.start()
        later_adapters()
        from_x[0].wait_recv()
        x_then_y.start()
        relay(0, 1)
        from_y[0].wait_recv()
        from_y[1].wait_recv()
        y_then_x.start()
        mate_y.start()
        relay(2)
        from_x[1].wait_recv()
        mate_x.start()
        relay(3)
        near_mid.wait_recv()
        add_base(near, everything, inner_at)
        relay(4, 5)
        remote(X_THEN_Y, spot(pd, 0), spot(pd, 0), groups=gy).wait_recv()
        mate_d0.start()
        remote(Y_THEN_X, spot(pd, 1), spot(pd, 1), replica=rx).wait_recv()
        mate_d1.start()
        relay(6, 7)
        partial_shrink()
        shrink_in.wait_recv()
        shr[2] = shr[0] + shr[1]
        shrink_mid.start()
        pc = g * 4 + rc
        remote(MATE, spot(pc), spot(pc), replica=rc).wait_recv()
        remote(MATE_X, spot(pc ^ 2), spot(pc ^ 2), replica=rc).wait_recv()
        remote(MATE_Y, spot(gy * 4 + rc), spot(gy * 4 + rc), replica=rc).wait_recv()
        qd = gy * 4 + (rc ^ 2)
        remote(MATE_D0, spot(qd, 0), spot(qd, 0), replica=rc).wait_recv()
        remote(MATE_D1, spot(qd, 1), spot(qd, 1), replica=rc).wait_recv()

        def put_near(cols, value):
            acc_h[:, cols] = value

        product(near, everything, help_w, pl.ds(0, depth), put_near)

        def help_edge(i):
            c, n = GROUPS[i]
            for at in range(c, c + n):
                forward[at].wait_recv()
            rows_of = group_rows[i]

            def put_far(cols, value):
                h_send[rows_of, cols] = (acc_h[rows_of, cols] + value).astype(jnp.bfloat16)

            product(distant, rows_of, help_w, pl.ds(depth, depth), put_far)
            helped[i].start()

        def finish(i):
            rows_of = group_rows[i]
            add_base(distant, rows_of, 3 - edge)
            out[rows_of, :] = acc[rows_of, :].astype(out.dtype)

        help_edge(0)
        shrink_mid.wait_recv()
        shr[4] = shr[2] + shr[3]
        shrink_out.start()
        add_base(outer, everything, edge)
        add_delta()
        help_edge(1)
        finish(0)
        help_edge(2)
        finish(1)
        help_edge(3)
        finish(2)
        finish(3)
        for copy in [near_mid, near_end, mate, x_then_y, y_then_x, shrink_mid, shrink_out]:
            copy.wait_send()
        for copy in along_x + along_y + [mate_x, mate_y, mate_d0, mate_d1] + forward + helped:
            copy.wait_send()

    for copy in adapters:
        copy.wait_send()


def shards_line4(tokens, query_weight, adapter_down, adapter_up, send_table, block_slot, live_block_rows):
    rows, depth = tokens.shape
    cols = query_weight.shape[1]
    rank = adapter_down.shape[2]
    adapter_down = adapter_down.transpose(0, 2, 1)
    bf16, f32 = jnp.bfloat16, jnp.float32
    any_space = pl.BlockSpec(memory_space=pl.ANY)
    vmem = pl.BlockSpec(memory_space=pltpu.VMEM)
    smem = pl.BlockSpec(memory_space=pltpu.SMEM)
    return pl.pallas_call(
        line4_kernel,
        out_shape=jax.ShapeDtypeStruct((rows, cols), bf16),
        in_specs=[any_space] * 4 + [smem] * 3,
        out_specs=vmem,
        scratch_shapes=[
            pltpu.VMEM((4 * depth, cols), bf16),
            pltpu.VMEM((2 * depth, cols), bf16),
            pltpu.VMEM((rows, depth), bf16),
            pltpu.VMEM((rows, depth), bf16),
            pltpu.VMEM((rows, depth), bf16),
            pltpu.VMEM((rows, depth), bf16),
            pltpu.VMEM((rows, cols), f32),
            pltpu.VMEM((rows, cols), f32),
            pltpu.VMEM((rows, cols), bf16),
            pltpu.VMEM((rows, cols), bf16),
            pltpu.VMEM((4, 2 * rank, depth), bf16),
            pltpu.VMEM((4, 2 * rank, cols), bf16),
            pltpu.VMEM((rows, 8 * rank), bf16),
            pltpu.VMEM((5, rows // 2, 128), f32),
            pltpu.VMEM((rows, 128), jnp.int32),
            pltpu.VMEM(adapter_down.shape, bf16),
            pltpu.VMEM(adapter_up.shape, bf16),
            pltpu.VMEM((3, 2 * rank, depth), bf16),
            pltpu.VMEM((3, 2 * rank, cols), bf16),
            pltpu.SemaphoreType.DMA((COPIES,)),
            pltpu.SemaphoreType.DMA((COPIES,)),
            pltpu.SemaphoreType.DMA((7,)),
        ],
        compiler_params=pltpu.CompilerParams(
            collective_id=0, has_side_effects=True, vmem_limit_bytes=60 << 20
        ),
        cost_estimate=pl.CostEstimate(flops=13 * 10**9, bytes_accessed=40 << 20, transcendentals=0),
    )(tokens, query_weight, adapter_down, adapter_up, send_table, block_slot, live_block_rows)


def solution(mesh):
    placed = (
        P(("groups", "replica"), "tensor"),
        P(None, "tensor"),
        P("replica", "tensor", None),
        P("replica", None, "tensor"),
        P("groups", None, None),
        P(("groups", "replica")),
        P(("groups", "replica")),
    )
    sizes = (mesh.shape["groups"], mesh.shape["replica"], mesh.shape["tensor"])
    body = shards_line4 if sizes == (2, 4, 4) else shards_any
    return jax.shard_map(
        body,
        mesh=mesh,
        in_specs=placed,
        out_specs=P(("groups", "replica"), "tensor"),
        check_vma=False,
    )
```

```python
import jax
import jax.numpy as jnp
from jax import lax
from jax.experimental import pallas as pl
from jax.experimental.pallas import tpu as pltpu
from jax.sharding import PartitionSpec as P

CHUNKS = 8
TILE = 256
GROUPS = ((0, 4), (4, 2), (6, 1), (7, 1))
MESH = pl.DeviceIdType.MESH

DOWN, UP, PIECE = 0, 3, 6
ALONG_X, ALONG_Y, MATE = 8, 10, 12
X_THEN_Y, Y_THEN_X = 13, 14
MATE_X, MATE_Y, MATE_D0, MATE_D1 = 15, 16, 17, 18
NEAR_END, NEAR_MID, SHRINK = 19, 20, 21
OUTER, FORWARD, HELPED = 24, 24 + CHUNKS, 24 + 2 * CHUNKS
COPIES = 24 + 3 * CHUNKS


def exchange_adapters(adapter_down, adapter_up, send_table):
    me = lax.axis_index("replica")
    count = lax.axis_size("replica")
    downs, ups = [], []
    for k in range(count):
        wanted = send_table[me, me ^ k]
        down = adapter_down[wanted]
        up = adapter_up[wanted]
        if k:
            perm = [(i, i ^ k) for i in range(count)]
            down = lax.ppermute(down, "replica", perm)
            up = lax.ppermute(up, "replica", perm)
        downs.append(down)
        ups.append(up)
    return downs, ups


def adapter_term(tokens, adapter_down, adapter_up, send_table, block_slot, live_block_rows):
    count = live_block_rows.shape[0]
    block_rows = tokens.shape[0] // count
    slots_each = send_table.shape[2]
    rank = adapter_down.shape[2]
    me = lax.axis_index("replica")
    downs, ups = exchange_adapters(adapter_down, adapter_up, send_table)
    place = ((block_slot // slots_each) ^ me) * slots_each + block_slot % slots_each
    row_place = jnp.repeat(place, block_rows)
    partial = jnp.zeros((tokens.shape[0], rank), jnp.float32)
    for k, down in enumerate(downs):
        product = jnp.einsum("rd,cdx->rcx", tokens, down, preferred_element_type=jnp.float32)
        for c in range(slots_each):
            partial = jnp.where((row_place == k * slots_each + c)[:, None], product[:, c], partial)
    shrink_round = lax.psum(partial, "tensor").astype(jnp.bfloat16)
    live = jnp.arange(block_rows, dtype=jnp.int32)[None, :] < live_block_rows[:, None]
    live = live.reshape(-1)
    pieces = len(downs) * slots_each
    spread = jnp.where(
        (live[:, None] & (row_place[:, None] == jnp.arange(pieces, dtype=jnp.int32)[None, :]))[:, :, None],
        shrink_round[:, None, :],
        jnp.bfloat16(0),
    ).reshape(tokens.shape[0], pieces * rank)
    up_all = jnp.concatenate(ups, axis=0).reshape(pieces * rank, -1)
    return jnp.dot(spread, up_all, preferred_element_type=jnp.float32)


def shards_any(tokens, query_weight, adapter_down, adapter_up, send_table, block_slot, live_block_rows):
    delta = adapter_term(tokens, adapter_down, adapter_up, send_table, block_slot, live_block_rows)
    base = jnp.dot(
        lax.all_gather(tokens, "tensor", axis=1, tiled=True),
        query_weight,
        preferred_element_type=jnp.float32,
    )
    return (base + delta).astype(jnp.bfloat16)


def line4_kernel(
    tokens, weight, adapter_down, adapter_up, send_table, block_slot, live_rows, out,
    w, help_w, own, near, outer, distant, acc, acc_h, h_send, h_recv, downs, ups, spread, shr,
    code, down_all, up_all, down_send, up_send, send, recv, local,
):
    g, r, t = lax.axis_index("groups"), lax.axis_index("replica"), lax.axis_index("tensor")
    rows, depth = own.shape
    step = rows // CHUNKS
    each = help_w.shape[0] // 8
    is_end = (t == 0) | (t == 3)
    is_mid = (t == 1) | (t == 2)
    inner = jnp.where(t < 2, t + 1, t - 1)
    edge = jnp.where(t < 2, 0, 3)
    other = 3 - t
    near_at = jnp.where(t < 2, 2, 1)
    far_at = jnp.where(t < 2, 3, 0)
    inner_at = jnp.where(is_end, inner, other)

    def remote(i, src, dst, **device_id):
        return pltpu.make_async_remote_copy(
            src_ref=src, dst_ref=dst, send_sem=send.at[i], recv_sem=recv.at[i],
            device_id=device_id, device_id_type=MESH,
        )

    def block(i):
        return pl.ds(pl.multiple_of(i * depth, depth), depth)

    def part(c):
        return pl.ds(c * step, step)

    def load_w(n, i):
        return pltpu.make_async_copy(weight.at[block(i)], w.at[block(i)], local.at[n])

    local_own = pltpu.make_async_copy(tokens, own, local.at[4])
    local_down = pltpu.make_async_copy(adapter_down, down_all, local.at[5])
    local_up = pltpu.make_async_copy(adapter_up, up_all, local.at[6])
    local_down.start()
    local_up.start()
    local_own.start()
    loads = [load_w(n, lax.rem(t + n, 4)) for n in range(4)]
    loads[0].start()

    barrier = pltpu.get_barrier_semaphore()
    for d in range(1, 4):
        pl.semaphore_signal(barrier, inc=1, device_id={"tensor": lax.rem(t + d, 4)}, device_id_type=MESH)
        pl.semaphore_signal(barrier, inc=1, device_id={"replica": r ^ d}, device_id_type=MESH)
    pl.semaphore_signal(barrier, inc=1, device_id={"groups": 1 - g}, device_id_type=MESH)
    pl.semaphore_wait(barrier, 7)

    peer = g * 4 + r

    def spot(p, half=None):
        if half is None:
            return help_w.at[pl.ds(pl.multiple_of(p * each, each), each)]
        return help_w.at[pl.ds(pl.multiple_of(p * each + half * (each // 2), each // 2), each // 2)]

    rx, gy, rc = r ^ 2, 1 - g, r ^ 1
    px, py, pd = g * 4 + rx, gy * 4 + r, gy * 4 + rx
    piece_row = jnp.where(g == 0, near_at, far_at) * depth + r * each
    half_piece = each // 2
    pieces = [
        remote(
            PIECE + h,
            weight.at[pl.ds(pl.multiple_of(piece_row + h * half_piece, half_piece), half_piece)],
            spot(peer, h),
            tensor=inner,
        )
        for h in range(2)
    ]
    along_x = [remote(ALONG_X + h, spot(peer, h), spot(peer, h), replica=rx) for h in range(2)]
    along_y = [remote(ALONG_Y + h, spot(peer, h), spot(peer, h), groups=gy) for h in range(2)]
    from_x = [remote(ALONG_X + h, spot(px, h), spot(px, h), replica=rx) for h in range(2)]
    from_y = [remote(ALONG_Y + h, spot(py, h), spot(py, h), groups=gy) for h in range(2)]
    mate = remote(MATE, spot(peer), spot(peer), replica=rc)
    x_then_y = remote(X_THEN_Y, spot(px, 0), spot(px, 0), groups=gy)
    y_then_x = remote(Y_THEN_X, spot(py, 1), spot(py, 1), replica=rx)
    mate_x = remote(MATE_X, spot(px), spot(px), replica=rc)
    mate_y = remote(MATE_Y, spot(py), spot(py), replica=rc)
    mate_d0 = remote(MATE_D0, spot(pd, 0), spot(pd, 0), replica=rc)
    mate_d1 = remote(MATE_D1, spot(pd, 1), spot(pd, 1), replica=rc)
    near_end = remote(NEAR_END, tokens, near, tensor=edge)
    near_mid = remote(NEAR_MID, tokens, near, tensor=other)
    to_inner = [remote(OUTER + c, tokens.at[part(c)], outer.at[part(c)], tensor=inner) for c in range(CHUNKS)]
    forward = [remote(FORWARD + c, outer.at[part(c)], distant.at[part(c)], tensor=other) for c in range(CHUNKS)]
    group_rows = [pl.ds(c * step, n * step) for c, n in GROUPS]
    helped = [
        remote(HELPED + i, h_send.at[rows_of], h_recv.at[rows_of], tensor=edge)
        for i, rows_of in enumerate(group_rows)
    ]
    adapters = []
    for k in (2, 3, 1):
        adapters.append(remote(DOWN + k - 1, down_send.at[k - 1], downs.at[k], replica=r ^ k))
        adapters.append(remote(UP + k - 1, up_send.at[k - 1], ups.at[k], replica=r ^ k))
    shrink_in = remote(SHRINK, shr.at[0], shr.at[1], tensor=inner)
    shrink_mid = remote(SHRINK + 1, shr.at[2], shr.at[3], tensor=other)
    shrink_out = remote(SHRINK + 2, shr.at[4], shr.at[4], tensor=edge)

    def product(x, x_rows, weights, w_rows, put):
        def tile(n, carry):
            cols = pl.ds(pl.multiple_of(n * TILE, TILE), TILE)
            put(cols, jnp.dot(x[x_rows, :], weights[w_rows, cols], preferred_element_type=jnp.float32))
            return carry

        lax.fori_loop(0, w.shape[1] // TILE, tile, 0)

    everything = pl.ds(0, rows)

    def add_base(x, x_rows, i):
        def put(cols, value):
            acc[x_rows, cols] += value

        product(x, x_rows, w, block(i), put)

    def own_base():
        local_own.wait()
        loads[0].wait()

        def put(cols, value):
            acc[:, cols] = value

        product(own, everything, w, block(t), put)

    low = lax.broadcasted_iota(jnp.int32, (rows, 128), 1) < 64

    def pick_adapters():
        local_down.wait()
        local_up.wait()
        for k in range(4):
            for c in range(2):
                wanted = send_table[r, r ^ k, c]
                down, up = down_all[wanted], up_all[wanted]
                if k:
                    down_send[k - 1, c * 64 : (c + 1) * 64] = down
                    up_send[k - 1, c * 64 : (c + 1) * 64] = up
                else:
                    downs[0, c * 64 : (c + 1) * 64] = down
                    ups[0, c * 64 : (c + 1) * 64] = up
        adapters[0].start()
        adapters[4].start()
        adapters[5].start()

    def later_adapters():
        for copy in adapters[1:4]:
            copy.start()

    def write_codes():
        count = block_slot.shape[0]
        size = rows // count
        row = lax.broadcasted_iota(jnp.int32, (size, 128), 0)
        for b in range(count):
            slot = block_slot[b]
            place = ((slot >> 1) ^ r) * 2 + (slot & 1)
            code[b * size : (b + 1) * size, :] = jnp.where(row < live_rows[b], place, -1)

    def partial_shrink():
        for copy in adapters:
            copy.wait_recv()
        total = jnp.zeros((rows, 128), jnp.float32)
        for k in range(4):
            value = lax.dot_general(
                own[...], downs[k], (((1,), (1,)), ((), ())), preferred_element_type=jnp.float32
            )
            hit = code[...] == jnp.where(low, 2 * k, 2 * k + 1)
            total = total + jnp.where(hit, value, 0.0)
        both = total + pltpu.roll(total, 64, 1)
        half = rows // 2
        shr[0] = jnp.where(low[:half], both[:half], both[half:])

    def add_delta():
        total = shr[4]
        turned = pltpu.roll(total, 64, 1)
        half = rows // 2
        top = low[:half]
        both = jnp.concatenate([jnp.where(top, total, turned), jnp.where(top, turned, total)], axis=0)
        for k in range(4):
            hit = code[...] == jnp.where(low, 2 * k, 2 * k + 1)
            spread[:, k * 128 : (k + 1) * 128] = jnp.where(hit, both, 0.0).astype(jnp.bfloat16)

        def tile(n, carry):
            cols = pl.ds(pl.multiple_of(n * TILE, TILE), TILE)
            value = jnp.zeros((rows, TILE), jnp.float32)
            for k in range(4):
                value = value + jnp.dot(
                    spread[:, k * 128 : (k + 1) * 128], ups[k, :, cols], preferred_element_type=jnp.float32
                )
            acc[:, cols] += value
            return carry

        lax.fori_loop(0, w.shape[1] // TILE, tile, 0)

    @pl.when(is_end)
    def _():
        pieces[0].start()
        pieces[1].start()

    @pl.when(is_mid)
    def _():
        near_mid.start()
        near_end.start()

    pick_adapters()
    for load in loads[1:]:
        load.start()
    write_codes()
    own_base()
    for load in loads[1:]:
        load.wait()

    @pl.when(is_end)
    def _():
        def follow(c):
            to_inner[c - 2].wait_send()
            to_inner[c].start()

        later_adapters()
        pieces[0].wait_send()
        to_inner[0].start()
        pieces[1].wait_send()
        to_inner[1].start()
        for c in range(2, CHUNKS - 2):
            follow(c)
        partial_shrink()
        shrink_in.start()
        for c in range(CHUNKS - 2, CHUNKS):
            follow(c)
        near_end.wait_recv()
        add_base(near, everything, inner_at)
        shrink_out.wait_recv()
        add_delta()
        for copy, rows_of in zip(helped, group_rows):
            copy.wait_recv()
            out[rows_of, :] = (acc[rows_of, :] + h_recv[rows_of, :].astype(jnp.float32)).astype(out.dtype)
        to_inner[CHUNKS - 2].wait_send()
        to_inner[CHUNKS - 1].wait_send()
        shrink_in.wait_send()

    @pl.when(is_mid)
    def _():
        def relay(*chunks):
            for c in chunks:
                to_inner[c].wait_recv()
                forward[c].start()

        for h in range(2):
            pieces[h].wait_recv()
            along_x[h].start()
            along_y[h].start()
        mate.start()
        later_adapters()
        from_x[0].wait_recv()
        x_then_y.start()
        relay(0, 1)
        from_y[0].wait_recv()
        from_y[1].wait_recv()
        y_then_x.start()
        mate_y.start()
        relay(2)
        from_x[1].wait_recv()
        mate_x.start()
        relay(3)
        near_mid.wait_recv()
        add_base(near, everything, inner_at)
        relay(4, 5)
        remote(X_THEN_Y, spot(pd, 0), spot(pd, 0), groups=gy).wait_recv()
        mate_d0.start()
        remote(Y_THEN_X, spot(pd, 1), spot(pd, 1), replica=rx).wait_recv()
        mate_d1.start()
        relay(6, 7)
        add_base(outer, everything, edge)
        pc = g * 4 + rc
        remote(MATE, spot(pc), spot(pc), replica=rc).wait_recv()
        remote(MATE_X, spot(pc ^ 2), spot(pc ^ 2), replica=rc).wait_recv()
        remote(MATE_Y, spot(gy * 4 + rc), spot(gy * 4 + rc), replica=rc).wait_recv()
        qd = gy * 4 + (rc ^ 2)
        remote(MATE_D0, spot(qd, 0), spot(qd, 0), replica=rc).wait_recv()
        remote(MATE_D1, spot(qd, 1), spot(qd, 1), replica=rc).wait_recv()

        def put_near(cols, value):
            acc_h[:, cols] = value

        product(near, everything, help_w, pl.ds(0, depth), put_near)

        def help_edge(i):
            c, n = GROUPS[i]
            for at in range(c, c + n):
                forward[at].wait_recv()
            rows_of = group_rows[i]

            def put_far(cols, value):
                h_send[rows_of, cols] = (acc_h[rows_of, cols] + value).astype(jnp.bfloat16)

            product(distant, rows_of, help_w, pl.ds(depth, depth), put_far)
            helped[i].start()

        def finish(i):
            rows_of = group_rows[i]
            add_base(distant, rows_of, 3 - edge)
            out[rows_of, :] = acc[rows_of, :].astype(out.dtype)

        partial_shrink()
        shrink_in.wait_recv()
        shr[2] = shr[0] + shr[1]
        shrink_mid.start()
        help_edge(0)
        add_base(distant, group_rows[0], 3 - edge)
        shrink_mid.wait_recv()
        shr[4] = shr[2] + shr[3]
        shrink_out.start()
        help_edge(1)
        add_delta()
        out[group_rows[0], :] = acc[group_rows[0], :].astype(out.dtype)
        help_edge(2)
        finish(1)
        help_edge(3)
        finish(2)
        finish(3)
        for copy in [near_mid, near_end, mate, x_then_y, y_then_x, shrink_mid, shrink_out]:
            copy.wait_send()
        for copy in along_x + along_y + [mate_x, mate_y, mate_d0, mate_d1] + forward + helped:
            copy.wait_send()

    for copy in adapters:
        copy.wait_send()


def shards_line4(tokens, query_weight, adapter_down, adapter_up, send_table, block_slot, live_block_rows):
    rows, depth = tokens.shape
    cols = query_weight.shape[1]
    rank = adapter_down.shape[2]
    adapter_down = adapter_down.transpose(0, 2, 1)
    bf16, f32 = jnp.bfloat16, jnp.float32
    any_space = pl.BlockSpec(memory_space=pl.ANY)
    vmem = pl.BlockSpec(memory_space=pltpu.VMEM)
    smem = pl.BlockSpec(memory_space=pltpu.SMEM)
    return pl.pallas_call(
        line4_kernel,
        out_shape=jax.ShapeDtypeStruct((rows, cols), bf16),
        in_specs=[any_space] * 4 + [smem] * 3,
        out_specs=vmem,
        scratch_shapes=[
            pltpu.VMEM((4 * depth, cols), bf16),
            pltpu.VMEM((2 * depth, cols), bf16),
            pltpu.VMEM((rows, depth), bf16),
            pltpu.VMEM((rows, depth), bf16),
            pltpu.VMEM((rows, depth), bf16),
            pltpu.VMEM((rows, depth), bf16),
            pltpu.VMEM((rows, cols), f32),
            pltpu.VMEM((rows, cols), f32),
            pltpu.VMEM((rows, cols), bf16),
            pltpu.VMEM((rows, cols), bf16),
            pltpu.VMEM((4, 2 * rank, depth), bf16),
            pltpu.VMEM((4, 2 * rank, cols), bf16),
            pltpu.VMEM((rows, 8 * rank), bf16),
            pltpu.VMEM((5, rows // 2, 128), f32),
            pltpu.VMEM((rows, 128), jnp.int32),
            pltpu.VMEM(adapter_down.shape, bf16),
            pltpu.VMEM(adapter_up.shape, bf16),
            pltpu.VMEM((3, 2 * rank, depth), bf16),
            pltpu.VMEM((3, 2 * rank, cols), bf16),
            pltpu.SemaphoreType.DMA((COPIES,)),
            pltpu.SemaphoreType.DMA((COPIES,)),
            pltpu.SemaphoreType.DMA((7,)),
        ],
        compiler_params=pltpu.CompilerParams(
            collective_id=0, has_side_effects=True, vmem_limit_bytes=60 << 20
        ),
        cost_estimate=pl.CostEstimate(flops=13 * 10**9, bytes_accessed=40 << 20, transcendentals=0),
    )(tokens, query_weight, adapter_down, adapter_up, send_table, block_slot, live_block_rows)


def solution(mesh):
    placed = (
        P(("groups", "replica"), "tensor"),
        P(None, "tensor"),
        P("replica", "tensor", None),
        P("replica", None, "tensor"),
        P("groups", None, None),
        P(("groups", "replica")),
        P(("groups", "replica")),
    )
    sizes = (mesh.shape["groups"], mesh.shape["replica"], mesh.shape["tensor"])
    body = shards_line4 if sizes == (2, 4, 4) else shards_any
    return jax.shard_map(
        body,
        mesh=mesh,
        in_specs=placed,
        out_specs=P(("groups", "replica"), "tensor"),
        check_vma=False,
    )
```
